32 devices in a mesh: ctx: 16 (over z, y, core), head: 2 (over x).
Axes of the slice: x: 2, y: 2, z: 4, core: 2. Of those that a mesh axis runs over, the one named last changes fastest.
Arguments:
- queries: bfloat16 [8192, 1024], P(('ctx', 'head')), may hold values from -9 to 9
- keys_in: bfloat16 [8192, 1024], P(('ctx', 'head')), may hold values from -9 to 9
- values: bfloat16 [8192, 1024], P(('ctx', 'head')), may hold values from -6 to 6
- d_out: bfloat16 [8192, 1024], P(('ctx', 'head')), may hold values from -6 to 6
- pair_blocks: int32 [128, 16], replicated, may hold values from 0 to 127, as said below
- pair_count: int32 [128], replicated, may hold values from 1 to 16, as said below
Outputs:
- d_queries: bfloat16 [8192, 1024], P(('ctx', 'head'))
- d_keys: bfloat16 [8192, 1024], P(('ctx', 'head'))
- d_values: bfloat16 [8192, 1024], P(('ctx', 'head'))
The draws below stay inside these ranges and needn't reach their ends.
Inputs may be any that keep to these rules, and one draw needn't show every extreme that they name: `pair_blocks`: entry 0 of row b is b itself; every entry of row b is a block of a person within 2 persons of the person of block b (a person's tokens are 512 in a row). Entries may repeat. Only the first pair_count[b] entries of row b are listed.
All inputs are finite; a program needn't handle non-finite values.
Results may differ from the reference program's by a relative error of at most 0.012.
The reference program's roundings to bfloat16 on the way (of `probs_b` and `d_scores`) count: a program that leaves them out, or rounds other values in their place, can miss the bound.
Values may be sent and summed in bfloat16 or wider, within the bound.
No kernel may reach another device: no remote copies, remote signals or barrier semaphores. Data moves between devices by JAX's collectives and lax.ppermute only.
A program may use at most 192 MiB of HBM per device.

```python
import jax
import jax.numpy as jnp
from jax import lax

HEADS = 16
HEAD_DIM = 64
FRAMES = 512
BLOCK = 64
REACH = 2
PAIRS = 16
PERSONS = 16
FEATURES = 1024
TOKENS = 8192


def query_key_pair(key):
    array_shape = (TOKENS, FEATURES)
    query_key = jax.random.fold_in(key, 101)
    key_key = jax.random.fold_in(key, 102)
    query_draw = jnp.clip(jax.random.normal(query_key, array_shape), -6.0, 6.0)
    key_draw = jnp.clip(jax.random.normal(key_key, array_shape), -6.0, 6.0)
    return (query_draw, key_draw)


def draw_queries(key, part):
    return query_key_pair(key)[0].astype(jnp.bfloat16)


def draw_keys_in(key, part):
    return query_key_pair(key)[1].astype(jnp.bfloat16)


def draw_pair_blocks(key, part):
    per_person = FRAMES // BLOCK
    total_blocks = PERSONS * per_person
    window_blocks = (2 * REACH + 1) * per_person
    block_ids = jnp.arange(total_blocks, dtype=jnp.int32)
    block_keys = jax.random.split(key, total_blocks)

    def one_block(block_key, block_id):
        person = block_id // per_person
        chosen_slots = jax.random.permutation(block_key, window_blocks - 1)[:PAIRS - 1].astype(jnp.int32)
        self_spot = REACH * per_person + block_id % per_person
        position = chosen_slots + (chosen_slots >= self_spot).astype(jnp.int32)
        offset = position // per_person - REACH
        target = person + offset
        offset = jnp.where((target < 0) | (target >= PERSONS), -offset, offset)
        picked = (person + offset) * per_person + position % per_person
        return jnp.concatenate([block_id[None], picked]).astype(jnp.int32)
    return jax.vmap(one_block)(block_keys, block_ids)


def draw_pair_count(key, part):
    per_person = FRAMES // BLOCK
    total_blocks = PERSONS * per_person
    busy_level = jax.random.randint(jax.random.fold_in(key, 1), (PERSONS,), 1, 5)
    drawn = jax.random.randint(jax.random.fold_in(key, 2), (total_blocks,), 1, PAIRS + 1)
    count_cap = jnp.maximum(1, busy_level * PAIRS // 4)
    counts = jnp.minimum(drawn, jnp.repeat(count_cap, per_person, total_repeat_length=total_blocks))
    full_block = jax.random.randint(jax.random.fold_in(key, 3), (), 0, total_blocks)
    return jnp.where(jnp.arange(total_blocks) == full_block, PAIRS, counts).astype(jnp.int32)


def block_scale(own_key, shape, shards, least, high):
    def one(dim, shards_of):
        heights = jax.random.uniform(jax.random.fold_in(jax.random.fold_in(own_key, 6), dim), (shards_of,), jnp.float32, least / len(shards), high / len(shards))
        return jnp.repeat(jnp.exp(heights), shape[dim] // shards_of).reshape((-1,) + (1,) * (len(shape) - dim - 1))

    factor_of = one(*shards[0])
    for cut in shards[1:]:
        factor_of = factor_of * one(*cut)
    return factor_of


def centred(own_key, dims, spread, bound, shards=(), kind=jnp.bfloat16):
    loudness = block_scale(own_key, dims, shards, -0.22, 0.18) if shards else 1.0
    result = jax.random.normal(own_key, dims, jnp.float32) * spread * loudness
    return jnp.minimum(jnp.maximum(result, -bound), bound).astype(kind)


def setup_inputs(seed: int = 0) -> dict:
    keys = jax.random.split(jax.random.key(seed), 7)
    queries = draw_queries(jax.random.fold_in(keys[6], 71), 0)
    keys_in = draw_keys_in(jax.random.fold_in(keys[6], 71), 0)
    values = centred(keys[2], (TOKENS, FEATURES), 1.0, 6.0, ((0, 32),))
    d_out = centred(keys[3], (TOKENS, FEATURES), 1.0, 6.0, ((0, 32),))
    pair_blocks = draw_pair_blocks(jax.random.fold_in(keys[6], 71), 0)
    pair_count = draw_pair_count(jax.random.fold_in(keys[6], 71), 0)
    return dict(queries=queries, keys_in=keys_in, values=values, d_out=d_out, pair_blocks=pair_blocks, pair_count=pair_count)


masked_value = -1.0e30


def reference(queries, keys_in, values, d_out, pair_blocks, pair_count):
    blocks_person = FRAMES // BLOCK
    window_span = 2 * REACH + 1
    window_rows = window_span * FRAMES
    margin = REACH * FRAMES
    score_scale = HEAD_DIM ** -0.5
    key_pad = jnp.pad(keys_in, ((margin, margin), (0, 0)))
    value_pad = jnp.pad(values, ((margin, margin), (0, 0)))
    live_slots = jnp.arange(PAIRS, dtype=jnp.int32)[None, :] < pair_count[:, None]

    def split_heads(matrix):
        return matrix.reshape(matrix.shape[0], HEADS, HEAD_DIM).astype(jnp.float32)

    def person_step(running, person):
        key_grad, value_grad = running
        start = (person * FRAMES).astype(jnp.int32)
        query_heads = split_heads(lax.dynamic_slice_in_dim(queries, start, FRAMES, 0))
        dout_heads = split_heads(lax.dynamic_slice_in_dim(d_out, start, FRAMES, 0))
        key_heads = split_heads(lax.dynamic_slice_in_dim(key_pad, start, window_rows, 0))
        value_heads = split_heads(lax.dynamic_slice_in_dim(value_pad, start, window_rows, 0))
        first = (person * blocks_person).astype(jnp.int32)
        lists = lax.dynamic_slice_in_dim(pair_blocks, first, blocks_person, 0)
        alive = lax.dynamic_slice_in_dim(live_slots, first, blocks_person, 0)
        wanted = ((person - REACH) * blocks_person).astype(jnp.int32) + jnp.arange(window_span * blocks_person, dtype=jnp.int32)
        block_mask = jnp.any((lists[:, :, None] == wanted[None, None, :]) & alive[:, :, None], axis=1)
        token_mask = jnp.broadcast_to(block_mask[:, None, :, None], (blocks_person, BLOCK, window_span * blocks_person, BLOCK)).reshape(FRAMES, window_rows)
        product = jnp.einsum("qhd,khd->hqk", query_heads, key_heads) * score_scale
        scores = jnp.where(token_mask[None], product, masked_value)
        row_top = jnp.max(scores, axis=-1, keepdims=True)
        row_total = jnp.sum(jnp.where(token_mask[None], jnp.exp(scores - row_top), 0.0), axis=-1, keepdims=True)
        log_total = row_top + jnp.log(row_total)
        probs = jnp.where(token_mask[None], jnp.exp(scores - log_total), 0.0)
        probs_b = lax.optimization_barrier(probs.astype(jnp.bfloat16)).astype(jnp.float32)
        attention = jnp.einsum("hqk,khd->qhd", probs_b, value_heads)
        row_delta = jnp.sum(dout_heads * attention, axis=-1).T
        d_probs = jnp.einsum("qhd,khd->hqk", dout_heads, value_heads)
        d_scores = lax.optimization_barrier((probs * (d_probs - row_delta[:, :, None])).astype(jnp.bfloat16)).astype(jnp.float32)
        query_grad = (jnp.einsum("hqk,khd->qhd", d_scores, key_heads) * score_scale).astype(jnp.bfloat16).reshape(FRAMES, FEATURES)
        key_part = jnp.einsum("hqk,qhd->khd", d_scores, query_heads).reshape(window_rows, FEATURES)
        value_part = jnp.einsum("hqk,qhd->khd", probs_b, dout_heads).reshape(window_rows, FEATURES)
        key_part = lax.optimization_barrier(key_part.astype(jnp.bfloat16)).astype(jnp.float32)
        value_part = lax.optimization_barrier(value_part.astype(jnp.bfloat16)).astype(jnp.float32)
        key_grad = lax.dynamic_update_slice_in_dim(key_grad, lax.dynamic_slice_in_dim(key_grad, start, window_rows, 0) + key_part, start, 0)
        value_grad = lax.dynamic_update_slice_in_dim(value_grad, lax.dynamic_slice_in_dim(value_grad, start, window_rows, 0) + value_part, start, 0)
        return (key_grad, value_grad), query_grad

    empty = jnp.zeros((TOKENS + 2 * margin, FEATURES), jnp.float32)
    (key_grad, value_grad), query_grads = lax.scan(person_step, (empty, empty), jnp.arange(PERSONS, dtype=jnp.int32))
    d_queries = query_grads.reshape(TOKENS, FEATURES)
    d_keys = (key_grad[margin:margin + TOKENS] * score_scale).astype(jnp.bfloat16)
    d_values = value_grad[margin:margin + TOKENS].astype(jnp.bfloat16)
    return (d_queries, d_keys, d_values)
```

```python
import jax
import jax.numpy as jnp
from jax import lax
from jax.experimental import pallas as pl
from jax.experimental.pallas import tpu as pltpu
from jax.sharding import Mesh
from jax.sharding import PartitionSpec as P

HEAD_DIM = 64
BLOCK = 64
REACH = 2
PERSONS_GROUP = 4
CHUNK = 2
STEP = 4
VMEM_BYTES = 63 * 1024 * 1024
LANES = 2 * HEAD_DIM
masked_value = -1e30


def dot_f32(lhs, rhs, lhs_dim, rhs_dim):
    return lax.dot_general(
        lhs, rhs, (((lhs_dim,), (rhs_dim,)), ((), ())), preferred_element_type=jnp.float32
    )


def mixed_rows(rows, mixer):
    return jnp.concatenate([rows] * 4, axis=0) * mixer[...]


def masked_softmax(both, live, slots, sure):
    biases = [jnp.where(slot < live, 0.0, masked_value) for slot in range(sure, slots)]
    scores = jnp.concatenate(
        [both[: sure * BLOCK, :LANES]]
        + [
            both[(sure + i) * BLOCK : (sure + i + 1) * BLOCK, :LANES] + bias
            for i, bias in enumerate(biases)
        ],
        axis=0,
    )
    d_probs = both[:, LANES:]
    top = jnp.max(scores, axis=0, keepdims=True)
    weights = jnp.exp(scores - top)
    inverse = 1.0 / jnp.sum(weights, axis=0, keepdims=True)
    delta = jnp.sum(weights * d_probs, axis=0, keepdims=True) * inverse
    probs = weights * inverse
    d_scores = probs * (d_probs - delta)
    return d_scores.astype(jnp.bfloat16), probs.astype(jnp.bfloat16)


def attend_step(slots, blocks, lives, lists_ref, qd, kv, acc, mixer, dq):
    rows = [pl.ds(pl.multiple_of(block * BLOCK, BLOCK), BLOCK) for block in blocks]
    places = [
        [
            pl.ds(pl.multiple_of(lists_ref[block, slot] * BLOCK, BLOCK), BLOCK)
            for slot in range(slots)
        ]
        for block in blocks
    ]
    weights = [mixed_rows(qd[row, :], mixer) for row in rows]
    windows = [jnp.concatenate([kv[place, :] for place in spot], axis=0) for spot in places]
    both = [dot_f32(window, weight, 1, 1) for window, weight in zip(windows, weights)]
    sures = [slots - CHUNK + 1] + [1] * (len(blocks) - 1)
    graded = [masked_softmax(b, live, slots, sure) for b, live, sure in zip(both, lives, sures)]
    grads = [
        dot_f32(jnp.concatenate([d_scores, probs], axis=1), weight, 1, 0)
        for (d_scores, probs), weight in zip(graded, weights)
    ]
    turned = [
        dot_f32(d_scores, window[:, :LANES], 0, 0)
        for (d_scores, _), window in zip(graded, windows)
    ]
    lane = lax.broadcasted_iota(jnp.int32, (BLOCK, LANES), 1)
    for row, both_heads in zip(rows, turned):
        picked = jnp.where(lane < HEAD_DIM, both_heads[:BLOCK], both_heads[BLOCK:])
        dq[row, :] = (picked * HEAD_DIM**-0.5).astype(jnp.bfloat16)
    for spot, grad in zip(places, grads):
        for slot, place in enumerate(spot):
            acc[place, :] += grad[slot * BLOCK : (slot + 1) * BLOCK]


def attend_kernel(
    lists_ref, counts_ref, order_ref, qd_ref, left_ref, own_ref, right_ref,
    dq_ref, grad_left, grad_own, grad_right,
    qd, kv, acc, mixer, dq, sems, dq_sems,
):
    pairs = lists_ref.shape[1]
    halo, own = grad_left.shape[0], grad_own.shape[0]
    spots = [pl.ds(0, halo), pl.ds(halo, own), pl.ds(halo + own, halo)]
    copies = [pltpu.make_async_copy(qd_ref, qd, sems.at[3])] + [
        pltpu.make_async_copy(ref, kv.at[spot, :], sems.at[i])
        for i, (ref, spot) in enumerate(zip((left_ref, own_ref, right_ref), spots))
    ]
    for copy in copies:
        copy.start()
    acc[...] = jnp.zeros_like(acc)
    group_row = lax.broadcasted_iota(jnp.int32, mixer.shape, 0) // HEAD_DIM
    group_lane = lax.broadcasted_iota(jnp.int32, mixer.shape, 1) // HEAD_DIM
    scale = jnp.where(group_row < 2, HEAD_DIM**-0.5, 1.0)
    mixer[...] = jnp.where(group_row == group_lane, scale, 0.0).astype(jnp.bfloat16)
    for copy in copies:
        copy.wait()

    def one_step(step, carry):
        blocks = [order_ref[STEP * step + i] for i in range(STEP)]
        lives = [counts_ref[block] for block in blocks]
        for chunks in range(1, pairs // CHUNK + 1):

            @pl.when((lives[0] + CHUNK - 1) // CHUNK == chunks)
            def _():
                attend_step(chunks * CHUNK, blocks, lives, lists_ref, qd, kv, acc, mixer, dq)

        return carry

    lax.fori_loop(0, counts_ref.shape[0] // STEP, one_step, 0)
    peers, rows, _ = dq_ref.shape
    backs = [
        pltpu.make_async_copy(dq.at[pl.ds(i * rows, rows), :], dq_ref.at[i], dq_sems.at[i])
        for i in range(peers)
    ]
    for back in backs:
        back.start()
    for i, (spot, ref) in enumerate(zip(spots, (grad_left, grad_own, grad_right))):
        kv[spot, :] = acc[spot, :].astype(jnp.bfloat16)
        back = pltpu.make_async_copy(kv.at[spot, :], ref, sems.at[i])
        back.start()
        backs.append(back)
    for back in backs:
        back.wait()


def attend(peers, lists, counts, order, qd, left, own, right):
    rows, halo = own.shape[0], left.shape[0]
    window = rows + 2 * halo
    scalars = pl.BlockSpec(memory_space=pltpu.SMEM)
    far = pl.BlockSpec(memory_space=pl.ANY)

    def shaped(shape):
        return jax.ShapeDtypeStruct(shape, jnp.bfloat16)

    return pl.pallas_call(
        attend_kernel,
        out_shape=(
            shaped((peers, rows // peers, LANES)),
            shaped((halo, 2 * LANES)),
            shaped((rows, 2 * LANES)),
            shaped((halo, 2 * LANES)),
        ),
        in_specs=[scalars, scalars, scalars, far, far, far, far],
        out_specs=(far, far, far, far),
        scratch_shapes=[
            pltpu.VMEM((rows, 2 * LANES), jnp.bfloat16),
            pltpu.VMEM((window, 2 * LANES), jnp.bfloat16),
            pltpu.VMEM((window, 2 * LANES), jnp.float32),
            pltpu.VMEM((2 * LANES, 2 * LANES), jnp.bfloat16),
            pltpu.VMEM((rows, LANES), jnp.bfloat16),
            pltpu.SemaphoreType.DMA((4,)),
            pltpu.SemaphoreType.DMA((peers,)),
        ],
        compiler_params=pltpu.CompilerParams(vmem_limit_bytes=VMEM_BYTES),
        cost_estimate=pl.CostEstimate(
            flops=4_000_000_000, bytes_accessed=6_000_000, transcendentals=2_000_000
        ),
        name="attend",
    )(lists, counts, order, qd, left, own, right)


def pack_kernel(first_ref, second_ref, joined_ref, packed, in_sems, out_sems):
    peers, _, width = joined_ref.shape
    width = width // 2
    arriving = [
        [
            pltpu.make_async_copy(
                ref.at[:, pl.ds(peer * width, width)],
                packed.at[peer, :, pl.ds(half * width, width)],
                in_sems.at[peer, half],
            )
            for half, ref in enumerate((first_ref, second_ref))
        ]
        for peer in range(peers)
    ]
    leaving = [
        pltpu.make_async_copy(packed.at[peer], joined_ref.at[peer], out_sems.at[peer])
        for peer in range(peers)
    ]
    for halves in arriving:
        for copy in halves:
            copy.start()
    for halves, out in zip(arriving, leaving):
        for copy in halves:
            copy.wait()
        out.start()
    for out in leaving:
        out.wait()


def join_columns(first, second, peers):
    rows, features = first.shape
    shape = (peers, rows, 2 * features // peers)
    anywhere = pl.BlockSpec(memory_space=pl.ANY)
    return pl.pallas_call(
        pack_kernel,
        out_shape=jax.ShapeDtypeStruct(shape, first.dtype),
        in_specs=[anywhere, anywhere],
        out_specs=anywhere,
        scratch_shapes=[
            pltpu.VMEM(shape, first.dtype),
            pltpu.SemaphoreType.DMA((peers, 2)),
            pltpu.SemaphoreType.DMA((peers,)),
        ],
        cost_estimate=pl.CostEstimate(flops=0, bytes_accessed=2_000_000, transcendentals=0),
        name="pack",
    )(first, second)


def compact_lists(pair_blocks, pair_count, first, rows, lowest, window_blocks):
    lists = lax.dynamic_slice_in_dim(pair_blocks, first, rows, 0) - lowest
    lists = jnp.clip(lists, 0, window_blocks - 1)
    counts = lax.dynamic_slice_in_dim(pair_count, first, rows, 0)
    slot = jnp.arange(lists.shape[1], dtype=jnp.int32)
    earlier = slot[None, :] < slot[:, None]
    repeat = jnp.any((lists[:, :, None] == lists[:, None, :]) & earlier[None], axis=2)
    keep = (slot[None, :] < counts[:, None]) & ~repeat
    place = jnp.sum(jnp.where(earlier[None], keep[:, None, :].astype(jnp.int32), 0), axis=2)
    chosen = keep[:, :, None] & (place[:, :, None] == slot[None, None, :])
    packed = jnp.sum(jnp.where(chosen, lists[:, :, None], 0), axis=1)
    lives = jnp.sum(keep.astype(jnp.int32), axis=1)
    block = jnp.arange(rows, dtype=jnp.int32)
    ahead = (lives[None, :] > lives[:, None]) | (
        (lives[None, :] == lives[:, None]) & (block[None, :] < block[:, None])
    )
    rank = jnp.sum(ahead.astype(jnp.int32), axis=1)
    order = jnp.sum(jnp.where(rank[:, None] == block[None, :], block[:, None], 0), axis=0)
    return packed, lives, order


def on_device(queries, keys_in, values, d_out, pair_blocks, pair_count):
    group = ("inner", "head")
    peers = lax.axis_size("inner") * lax.axis_size("head")
    outer = lax.axis_size("outer")
    tokens_dev, features = queries.shape
    tokens = tokens_dev * peers
    halo = REACH * (tokens // PERSONS_GROUP)
    blocks, halo_blocks = tokens // BLOCK, halo // BLOCK

    def exchange(parts):
        return lax.all_to_all(parts, group, split_axis=0, concat_axis=0, tiled=True)

    up = [(i, i + 1) for i in range(outer - 1)]
    down = [(i + 1, i) for i in range(outer - 1)]
    own = exchange(join_columns(keys_in, values, peers))
    edge = halo // tokens_dev
    left = lax.ppermute(own[peers - edge :], "outer", up).reshape(halo, 2 * LANES)
    right = lax.ppermute(own[:edge], "outer", down).reshape(halo, 2 * LANES)
    own = own.reshape(tokens, 2 * LANES)
    qd = exchange(join_columns(queries, d_out, peers)).reshape(tokens, 2 * LANES)
    first = lax.axis_index("outer") * blocks
    lists, counts, order = compact_lists(
        pair_blocks, pair_count, first, blocks, first - halo_blocks, blocks + 2 * halo_blocks
    )
    dq, grad_left, grad_own, grad_right = attend(
        peers, lists, counts, order, qd, left, own, right
    )
    from_above = lax.ppermute(grad_left, "outer", down)
    from_below = lax.ppermute(grad_right, "outer", up)
    dq_back = exchange(dq)
    arrived = jnp.concatenate([from_below, from_above], axis=0)
    total = (grad_own.astype(jnp.float32) + arrived.astype(jnp.float32)).astype(jnp.bfloat16)
    grads = exchange(total.reshape(peers, tokens_dev, 2 * LANES))

    def columns(parts):
        return parts.transpose(1, 0, 2).reshape(tokens_dev, features)

    return columns(dq_back), columns(grads[:, :, :LANES]), columns(grads[:, :, LANES:])


def solution(mesh):
    ctx, head = mesh.devices.shape
    grouped = Mesh(
        mesh.devices.reshape(ctx // PERSONS_GROUP, PERSONS_GROUP, head), ("outer", "inner", "head")
    )
    rows = P(("outer", "inner", "head"), None)
    return jax.shard_map(
        on_device,
        mesh=grouped,
        in_specs=(rows, rows, rows, rows, P(), P()),
        out_specs=(rows, rows, rows),
        check_vma=False,
    )
```

```python
import jax
import jax.numpy as jnp
from jax import lax
from jax.experimental import pallas as pl
from jax.experimental.pallas import tpu as pltpu
from jax.sharding import Mesh
from jax.sharding import PartitionSpec as P

HEAD_DIM = 64
BLOCK = 64
REACH = 2
PERSONS_GROUP = 4
CHUNK = 4
STEP = 4
SENDS = (5, 6, 1, 7, 4, 3, 2)
VMEM_BYTES = 63 * 1024 * 1024
LANES = 2 * HEAD_DIM
masked_value = -1e30


def dot_f32(lhs, rhs, lhs_dim, rhs_dim):
    return lax.dot_general(
        lhs, rhs, (((lhs_dim,), (rhs_dim,)), ((), ())), preferred_element_type=jnp.float32
    )


def mixed_rows(rows, mixer):
    return jnp.concatenate([rows] * 4, axis=0) * mixer[...]


def masked_softmax(both, live, slots, sure):
    biases = [jnp.where(slot < live, 0.0, masked_value) for slot in range(sure, slots)]
    scores = jnp.concatenate(
        [both[: sure * BLOCK, :LANES]]
        + [
            both[(sure + i) * BLOCK : (sure + i + 1) * BLOCK, :LANES] + bias
            for i, bias in enumerate(biases)
        ],
        axis=0,
    )
    d_probs = both[:, LANES:]
    top = jnp.max(scores, axis=0, keepdims=True)
    weights = jnp.exp(scores - top)
    inverse = 1.0 / jnp.sum(weights, axis=0, keepdims=True)
    delta = jnp.sum(weights * d_probs, axis=0, keepdims=True) * inverse
    probs = weights * inverse
    d_scores = probs * (d_probs - delta)
    return d_scores.astype(jnp.bfloat16), probs.astype(jnp.bfloat16)


def attend_step(slots, blocks, lives, lists_ref, qd, kv, acc, mixer, dq):
    rows = [pl.ds(pl.multiple_of(block * BLOCK, BLOCK), BLOCK) for block in blocks]
    places = [
        [
            pl.ds(pl.multiple_of(lists_ref[block, slot] * BLOCK, BLOCK), BLOCK)
            for slot in range(slots)
        ]
        for block in blocks
    ]
    weights = [mixed_rows(qd[row, :], mixer) for row in rows]
    windows = [jnp.concatenate([kv[place, :] for place in spot], axis=0) for spot in places]
    both = [dot_f32(window, weight, 1, 1) for window, weight in zip(windows, weights)]
    sures = [slots - CHUNK + 1] + [1] * (len(blocks) - 1)
    graded = [masked_softmax(b, live, slots, sure) for b, live, sure in zip(both, lives, sures)]
    grads = [
        dot_f32(jnp.concatenate([d_scores, probs], axis=1), weight, 1, 0)
        for (d_scores, probs), weight in zip(graded, weights)
    ]
    turned = [
        dot_f32(d_scores, window[:, :LANES], 0, 0)
        for (d_scores, _), window in zip(graded, windows)
    ]
    lane = lax.broadcasted_iota(jnp.int32, (BLOCK, LANES), 1)
    for row, both_heads in zip(rows, turned):
        picked = jnp.where(lane < HEAD_DIM, both_heads[:BLOCK], both_heads[BLOCK:])
        dq[row, :] = (picked * HEAD_DIM**-0.5).astype(jnp.bfloat16)
    for spot, grad in zip(places, grads):
        for slot, place in enumerate(spot):
            acc[place, :] += grad[slot * BLOCK : (slot + 1) * BLOCK]


def attend_kernel(
    me_ref, lists_ref, counts_ref, order_ref, *refs
):
    peers = len(refs) // 2 - 7
    qd_refs, own_refs = refs[:peers], refs[peers : 2 * peers]
    near_ref, across_ref, dq_ref, grad_left, grad_own, grad_right = refs[2 * peers : 2 * peers + 6]
    qd, kv, acc, mixer, dq, in_sems, sems, dq_sems = refs[2 * peers + 6 :]
    pairs = lists_ref.shape[1]
    halo, own = grad_left.shape[0], grad_own.shape[0]
    spots = [pl.ds(0, halo), pl.ds(halo, own), pl.ds(halo + own, halo)]
    me = me_ref[0]
    piece = own_refs[0].shape[0]
    edge = halo // piece
    lower = me < edge

    def rows_at(base, slab):
        return pl.ds(pl.multiple_of(base + slab * piece, piece), piece)

    copies = []
    for k in range(peers):
        spot = rows_at(0, me ^ k)
        copies.append(pltpu.make_async_copy(qd_refs[k], qd.at[spot, :], in_sems.at[0, k]))
        spot = rows_at(halo, me ^ k)
        copies.append(pltpu.make_async_copy(own_refs[k], kv.at[spot, :], in_sems.at[1, k]))
    for k in range(edge):
        spot = rows_at(jnp.where(lower, halo + own, 0), (me ^ k) % edge)
        copies.append(pltpu.make_async_copy(near_ref.at[k], kv.at[spot, :], in_sems.at[2, k]))
        spot = rows_at(jnp.where(lower, 0, halo + own), (me ^ k) % edge)
        copies.append(
            pltpu.make_async_copy(across_ref.at[k], kv.at[spot, :], in_sems.at[2, edge + k])
        )
    for copy in copies:
        copy.start()
    acc[...] = jnp.zeros_like(acc)
    group_row = lax.broadcasted_iota(jnp.int32, mixer.shape, 0) // HEAD_DIM
    group_lane = lax.broadcasted_iota(jnp.int32, mixer.shape, 1) // HEAD_DIM
    scale = jnp.where(group_row < 2, HEAD_DIM**-0.5, 1.0)
    mixer[...] = jnp.where(group_row == group_lane, scale, 0.0).astype(jnp.bfloat16)
    for copy in copies:
        copy.wait()

    def one_step(step, carry):
        blocks = [order_ref[STEP * step + i] for i in range(STEP)]
        lives = [counts_ref[block] for block in blocks]
        for chunks in range(1, pairs // CHUNK + 1):

            @pl.when((lives[0] + CHUNK - 1) // CHUNK == chunks)
            def _():
                attend_step(chunks * CHUNK, blocks, lives, lists_ref, qd, kv, acc, mixer, dq)

        return carry

    lax.fori_loop(0, counts_ref.shape[0] // STEP, one_step, 0)
    rows = dq_ref.shape[1]
    backs = [
        pltpu.make_async_copy(dq.at[pl.ds(i * rows, rows), :], dq_ref.at[i], dq_sems.at[i])
        for i in range(peers)
    ]
    for back in backs:
        back.start()
    for i, (spot, ref) in enumerate(zip(spots, (grad_left, grad_own, grad_right))):
        kv[spot, :] = acc[spot, :].astype(jnp.bfloat16)
        back = pltpu.make_async_copy(kv.at[spot, :], ref, sems.at[i])
        back.start()
        backs.append(back)
    for back in backs:
        back.wait()


def attend(me, lists, counts, order, qd, own, near, across):
    peers, piece = len(own), own[0].shape[0]
    rows, halo = peers * piece, near.shape[0] * piece
    window = rows + 2 * halo
    scalars = pl.BlockSpec(memory_space=pltpu.SMEM)
    far = pl.BlockSpec(memory_space=pl.ANY)

    def shaped(shape):
        return jax.ShapeDtypeStruct(shape, jnp.bfloat16)

    return pl.pallas_call(
        attend_kernel,
        out_shape=(
            shaped((peers, rows // peers, LANES)),
            shaped((halo, 2 * LANES)),
            shaped((rows, 2 * LANES)),
            shaped((halo, 2 * LANES)),
        ),
        in_specs=[scalars] * 4 + [far] * (2 * peers + 2),
        out_specs=(far, far, far, far),
        scratch_shapes=[
            pltpu.VMEM((rows, 2 * LANES), jnp.bfloat16),
            pltpu.VMEM((window, 2 * LANES), jnp.bfloat16),
            pltpu.VMEM((window, 2 * LANES), jnp.float32),
            pltpu.VMEM((2 * LANES, 2 * LANES), jnp.bfloat16),
            pltpu.VMEM((rows, LANES), jnp.bfloat16),
            pltpu.SemaphoreType.DMA((3, peers)),
            pltpu.SemaphoreType.DMA((3,)),
            pltpu.SemaphoreType.DMA((peers,)),
        ],
        compiler_params=pltpu.CompilerParams(vmem_limit_bytes=VMEM_BYTES),
        cost_estimate=pl.CostEstimate(
            flops=4_000_000_000, bytes_accessed=6_000_000, transcendentals=2_000_000
        ),
        name="attend",
    )(me, lists, counts, order, *qd, *own, near, across)


def pack_kernel(me_ref, first_ref, second_ref, *refs):
    joined_refs, (packed, in_sems, out_sems) = refs[:-3], refs[-3:]
    peers, _, width = packed.shape
    width = width // 2
    me = me_ref[0]
    arriving = [
        [
            pltpu.make_async_copy(
                ref.at[:, pl.ds(pl.multiple_of((me ^ slab) * width, width), width)],
                packed.at[slab, :, pl.ds(half * width, width)],
                in_sems.at[slab, half],
            )
            for half, ref in enumerate((first_ref, second_ref))
        ]
        for slab in range(peers)
    ]
    leaving = [
        pltpu.make_async_copy(packed.at[slab], joined_refs[slab], out_sems.at[slab])
        for slab in range(peers)
    ]
    for halves in arriving:
        for copy in halves:
            copy.start()
    for halves, out in zip(arriving, leaving):
        for copy in halves:
            copy.wait()
        out.start()
    for out in leaving:
        out.wait()


def join_columns(me, first, second, peers):
    rows, features = first.shape
    shape = (peers, rows, 2 * features // peers)
    anywhere = pl.BlockSpec(memory_space=pl.ANY)
    slab = jax.ShapeDtypeStruct(shape[1:], first.dtype)
    return pl.pallas_call(
        pack_kernel,
        out_shape=[slab] * peers,
        in_specs=[pl.BlockSpec(memory_space=pltpu.SMEM), anywhere, anywhere],
        out_specs=[anywhere] * peers,
        scratch_shapes=[
            pltpu.VMEM(shape, first.dtype),
            pltpu.SemaphoreType.DMA((peers, 2)),
            pltpu.SemaphoreType.DMA((peers,)),
        ],
        cost_estimate=pl.CostEstimate(flops=0, bytes_accessed=2_000_000, transcendentals=0),
        name="pack",
    )(me, first, second)


def compact_lists(pair_blocks, pair_count, first, rows, lowest, window_blocks):
    lists = lax.dynamic_slice_in_dim(pair_blocks, first, rows, 0) - lowest
    lists = jnp.clip(lists, 0, window_blocks - 1)
    counts = lax.dynamic_slice_in_dim(pair_count, first, rows, 0)
    slot = jnp.arange(lists.shape[1], dtype=jnp.int32)
    earlier = slot[None, :] < slot[:, None]
    repeat = jnp.any((lists[:, :, None] == lists[:, None, :]) & earlier[None], axis=2)
    keep = (slot[None, :] < counts[:, None]) & ~repeat
    place = jnp.sum(jnp.where(earlier[None], keep[:, None, :].astype(jnp.int32), 0), axis=2)
    chosen = keep[:, :, None] & (place[:, :, None] == slot[None, None, :])
    packed = jnp.sum(jnp.where(chosen, lists[:, :, None], 0), axis=1)
    lives = jnp.sum(keep.astype(jnp.int32), axis=1)
    block = jnp.arange(rows, dtype=jnp.int32)
    ahead = (lives[None, :] > lives[:, None]) | (
        (lives[None, :] == lives[:, None]) & (block[None, :] < block[:, None])
    )
    rank = jnp.sum(ahead.astype(jnp.int32), axis=1)
    order = jnp.sum(jnp.where(rank[:, None] == block[None, :], block[:, None], 0), axis=0)
    return packed, lives, order


def on_device(queries, keys_in, values, d_out, pair_blocks, pair_count):
    group = ("inner", "head")
    peers = lax.axis_size("inner") * lax.axis_size("head")
    outer = lax.axis_size("outer")
    tokens_dev, features = queries.shape
    tokens = tokens_dev * peers
    halo = REACH * (tokens // PERSONS_GROUP)
    blocks, halo_blocks = tokens // BLOCK, halo // BLOCK

    def exchange(parts):
        return lax.all_to_all(parts, group, split_axis=0, concat_axis=0, tiled=True)

    me = lax.axis_index(group)
    my_slab = me.astype(jnp.int32).reshape(1)
    half = peers // 2

    def send(slab, k):
        return lax.ppermute(slab, group, [(i, i ^ k) for i in range(peers)])

    def scatter(slabs):
        moved = {k: send(slabs[k], k) for k in SENDS}
        return [slabs[0]] + [moved[k] for k in range(1, peers)]

    def beside(slabs, lower, upper):
        pairs = [
            (o * peers + i, (o + (lower if i < half else upper)) * peers + i)
            for o in range(outer)
            for i in range(peers)
            if 0 <= o + (lower if i < half else upper) < outer
        ]
        return lax.ppermute(slabs, ("outer",) + group, pairs)

    up = [(i, i + 1) for i in range(outer - 1)]
    down = [(i + 1, i) for i in range(outer - 1)]
    own = scatter(join_columns(my_slab, keys_in, values, peers))
    qd = scatter(join_columns(my_slab, queries, d_out, peers))
    near = beside(jnp.stack(own[:half]), -1, 1)
    across = beside(jnp.stack(own[half:]), 1, -1)
    first = lax.axis_index("outer") * blocks
    lists, counts, order = compact_lists(
        pair_blocks, pair_count, first, blocks, first - halo_blocks, blocks + 2 * halo_blocks
    )
    dq, grad_left, grad_own, grad_right = attend(
        my_slab, lists, counts, order, qd, own, near, across
    )
    from_above = lax.ppermute(grad_left, "outer", down)
    from_below = lax.ppermute(grad_right, "outer", up)
    dq_back = exchange(dq)
    arrived = jnp.concatenate([from_below, from_above], axis=0)
    total = (grad_own.astype(jnp.float32) + arrived.astype(jnp.float32)).astype(jnp.bfloat16)
    grads = exchange(total.reshape(peers, tokens_dev, 2 * LANES))

    def columns(parts):
        return parts.transpose(1, 0, 2).reshape(tokens_dev, features)

    return columns(dq_back), columns(grads[:, :, :LANES]), columns(grads[:, :, LANES:])


def solution(mesh):
    ctx, head = mesh.devices.shape
    grouped = Mesh(
        mesh.devices.reshape(ctx // PERSONS_GROUP, PERSONS_GROUP, head), ("outer", "inner", "head")
    )
    rows = P(("outer", "inner", "head"), None)
    return jax.shard_map(
        on_device,
        mesh=grouped,
        in_specs=(rows, rows, rows, rows, P(), P()),
        out_specs=(rows, rows, rows),
        check_vma=False,
    )
```

```python
import jax
import jax.numpy as jnp
from jax import lax
from jax.experimental import pallas as pl
from jax.experimental.pallas import tpu as pltpu
from jax.sharding import Mesh
from jax.sharding import PartitionSpec as P

HEAD_DIM = 64
BLOCK = 64
REACH = 2
PERSONS_GROUP = 4
CHUNK = 4
STEP = 4
SENDS = (4, 1, 5, 6, 3, 7, 2)
VMEM_BYTES = 63 * 1024 * 1024
LANES = 2 * HEAD_DIM
masked_value = -1e30


def dot_f32(lhs, rhs, lhs_dim, rhs_dim):
    return lax.dot_general(
        lhs, rhs, (((lhs_dim,), (rhs_dim,)), ((), ())), preferred_element_type=jnp.float32
    )


def mixed_rows(rows, mixer):
    return jnp.concatenate([rows] * 4, axis=0) * mixer[...]


def masked_softmax(both, live, slots, sure):
    biases = [jnp.where(slot < live, 0.0, masked_value) for slot in range(sure, slots)]
    scores = jnp.concatenate(
        [both[: sure * BLOCK, :LANES]]
        + [
            both[(sure + i) * BLOCK : (sure + i + 1) * BLOCK, :LANES] + bias
            for i, bias in enumerate(biases)
        ],
        axis=0,
    )
    d_probs = both[:, LANES:]
    top = jnp.max(scores, axis=0, keepdims=True)
    weights = jnp.exp(scores - top)
    inverse = 1.0 / jnp.sum(weights, axis=0, keepdims=True)
    delta = jnp.sum(weights * d_probs, axis=0, keepdims=True) * inverse
    probs = weights * inverse
    d_scores = probs * (d_probs - delta)
    return d_scores.astype(jnp.bfloat16), probs.astype(jnp.bfloat16)


def attend_step(slots, blocks, lives, lists_ref, qd, kv, acc, mixer, dq):
    rows = [pl.ds(pl.multiple_of(block * BLOCK, BLOCK), BLOCK) for block in blocks]
    places = [
        [
            pl.ds(pl.multiple_of(lists_ref[block, slot] * BLOCK, BLOCK), BLOCK)
            for slot in range(slots)
        ]
        for block in blocks
    ]
    weights = [mixed_rows(qd[row, :], mixer) for row in rows]
    windows = [jnp.concatenate([kv[place, :] for place in spot], axis=0) for spot in places]
    both = [dot_f32(window, weight, 1, 1) for window, weight in zip(windows, weights)]
    sures = [slots - CHUNK + 1] + [1] * (len(blocks) - 1)
    graded = [masked_softmax(b, live, slots, sure) for b, live, sure in zip(both, lives, sures)]
    grads = [
        dot_f32(jnp.concatenate([d_scores, probs], axis=1), weight, 1, 0)
        for (d_scores, probs), weight in zip(graded, weights)
    ]
    turned = [
        dot_f32(d_scores, window[:, :LANES], 0, 0)
        for (d_scores, _), window in zip(graded, windows)
    ]
    lane = lax.broadcasted_iota(jnp.int32, (BLOCK, LANES), 1)
    for row, both_heads in zip(rows, turned):
        picked = jnp.where(lane < HEAD_DIM, both_heads[:BLOCK], both_heads[BLOCK:])
        dq[row, :] = (picked * HEAD_DIM**-0.5).astype(jnp.bfloat16)
    for spot, grad in zip(places, grads):
        for slot, place in enumerate(spot):
            acc[place, :] += grad[slot * BLOCK : (slot + 1) * BLOCK]


def attend_kernel(
    me_ref, lists_ref, counts_ref, order_ref, *refs
):
    peers = len(refs) // 2 - 7
    qd_refs, own_refs = refs[:peers], refs[peers : 2 * peers]
    near_ref, across_ref, dq_ref, grad_left, grad_own, grad_right = refs[2 * peers : 2 * peers + 6]
    qd, kv, acc, mixer, dq, in_sems, sems, dq_sems = refs[2 * peers + 6 :]
    pairs = lists_ref.shape[1]
    halo, own = grad_left.shape[0], grad_own.shape[0]
    spots = [pl.ds(0, halo), pl.ds(halo, own), pl.ds(halo + own, halo)]
    me = me_ref[0]
    piece = own_refs[0].shape[0]
    edge = halo // piece
    lower = me < edge

    def rows_at(base, slab):
        return pl.ds(pl.multiple_of(base + slab * piece, piece), piece)

    copies = []
    for place, k in enumerate((0,) + SENDS):
        spot = rows_at(0, me ^ k)
        copies.append(pltpu.make_async_copy(qd_refs[place], qd.at[spot, :], in_sems.at[0, k]))
        spot = rows_at(halo, me ^ k)
        copies.append(pltpu.make_async_copy(own_refs[place], kv.at[spot, :], in_sems.at[1, k]))
    for k in range(edge):
        spot = rows_at(jnp.where(lower, halo + own, 0), (me ^ k) % edge)
        copies.append(pltpu.make_async_copy(near_ref.at[k], kv.at[spot, :], in_sems.at[2, k]))
        spot = rows_at(jnp.where(lower, 0, halo + own), (me ^ k) % edge)
        copies.append(
            pltpu.make_async_copy(across_ref.at[k], kv.at[spot, :], in_sems.at[2, edge + k])
        )
    for copy in copies:
        copy.start()
    acc[...] = jnp.zeros_like(acc)
    group_row = lax.broadcasted_iota(jnp.int32, mixer.shape, 0) // HEAD_DIM
    group_lane = lax.broadcasted_iota(jnp.int32, mixer.shape, 1) // HEAD_DIM
    scale = jnp.where(group_row < 2, HEAD_DIM**-0.5, 1.0)
    mixer[...] = jnp.where(group_row == group_lane, scale, 0.0).astype(jnp.bfloat16)
    for copy in copies:
        copy.wait()

    def one_step(step, carry):
        blocks = [order_ref[STEP * step + i] for i in range(STEP)]
        lives = [counts_ref[block] for block in blocks]
        for chunks in range(1, pairs // CHUNK + 1):

            @pl.when((lives[0] + CHUNK - 1) // CHUNK == chunks)
            def _():
                attend_step(chunks * CHUNK, blocks, lives, lists_ref, qd, kv, acc, mixer, dq)

        return carry

    lax.fori_loop(0, counts_ref.shape[0] // STEP, one_step, 0)
    rows = dq_ref.shape[1]
    backs = [
        pltpu.make_async_copy(dq.at[pl.ds(i * rows, rows), :], dq_ref.at[i], dq_sems.at[i])
        for i in range(peers)
    ]
    for back in backs:
        back.start()
    for i, (spot, ref) in enumerate(zip(spots, (grad_left, grad_own, grad_right))):
        kv[spot, :] = acc[spot, :].astype(jnp.bfloat16)
        back = pltpu.make_async_copy(kv.at[spot, :], ref, sems.at[i])
        back.start()
        backs.append(back)
    for back in backs:
        back.wait()


def attend(me, lists, counts, order, qd, own, near, across):
    peers, piece = len(own), own[0].shape[0]
    rows, halo = peers * piece, near.shape[0] * piece
    window = rows + 2 * halo
    scalars = pl.BlockSpec(memory_space=pltpu.SMEM)
    far = pl.BlockSpec(memory_space=pl.ANY)

    def shaped(shape):
        return jax.ShapeDtypeStruct(shape, jnp.bfloat16)

    return pl.pallas_call(
        attend_kernel,
        out_shape=(
            shaped((peers, rows // peers, LANES)),
            shaped((halo, 2 * LANES)),
            shaped((rows, 2 * LANES)),
            shaped((halo, 2 * LANES)),
        ),
        in_specs=[scalars] * 4 + [far] * (2 * peers + 2),
        out_specs=(far, far, far, far),
        scratch_shapes=[
            pltpu.VMEM((rows, 2 * LANES), jnp.bfloat16),
            pltpu.VMEM((window, 2 * LANES), jnp.bfloat16),
            pltpu.VMEM((window, 2 * LANES), jnp.float32),
            pltpu.VMEM((2 * LANES, 2 * LANES), jnp.bfloat16),
            pltpu.VMEM((rows, LANES), jnp.bfloat16),
            pltpu.SemaphoreType.DMA((3, peers)),
            pltpu.SemaphoreType.DMA((3,)),
            pltpu.SemaphoreType.DMA((peers,)),
        ],
        compiler_params=pltpu.CompilerParams(vmem_limit_bytes=VMEM_BYTES),
        cost_estimate=pl.CostEstimate(
            flops=4_000_000_000, bytes_accessed=6_000_000, transcendentals=2_000_000
        ),
        name="attend",
    )(me, lists, counts, order, *qd, *own, near, across)


def pack_kernel(me_ref, first_ref, second_ref, *refs):
    joined_refs, (packed, in_sems, out_sems) = refs[:-3], refs[-3:]
    peers, _, width = packed.shape
    width = width // 2
    me = me_ref[0]
    arriving = [
        [
            pltpu.make_async_copy(
                ref.at[:, pl.ds(pl.multiple_of((me ^ slab) * width, width), width)],
                packed.at[slab, :, pl.ds(half * width, width)],
                in_sems.at[slab, half],
            )
            for half, ref in enumerate((first_ref, second_ref))
        ]
        for slab in range(peers)
    ]
    leaving = [
        pltpu.make_async_copy(packed.at[slab], joined_refs[slab], out_sems.at[slab])
        for slab in range(peers)
    ]
    for halves in arriving:
        for copy in halves:
            copy.start()
    for halves, out in zip(arriving, leaving):
        for copy in halves:
            copy.wait()
        out.start()
    for out in leaving:
        out.wait()


def join_columns(me, first, second, peers):
    rows, features = first.shape
    shape = (peers, rows, 2 * features // peers)
    anywhere = pl.BlockSpec(memory_space=pl.ANY)
    slab = jax.ShapeDtypeStruct(shape[1:], first.dtype)
    return pl.pallas_call(
        pack_kernel,
        out_shape=[slab] * peers,
        in_specs=[pl.BlockSpec(memory_space=pltpu.SMEM), anywhere, anywhere],
        out_specs=[anywhere] * peers,
        scratch_shapes=[
            pltpu.VMEM(shape, first.dtype),
            pltpu.SemaphoreType.DMA((peers, 2)),
            pltpu.SemaphoreType.DMA((peers,)),
        ],
        cost_estimate=pl.CostEstimate(flops=0, bytes_accessed=2_000_000, transcendentals=0),
        name="pack",
    )(me, first, second)


def compact_lists(pair_blocks, pair_count, first, rows, lowest, window_blocks):
    lists = lax.dynamic_slice_in_dim(pair_blocks, first, rows, 0) - lowest
    lists = jnp.clip(lists, 0, window_blocks - 1)
    counts = lax.dynamic_slice_in_dim(pair_count, first, rows, 0)
    slot = jnp.arange(lists.shape[1], dtype=jnp.int32)
    earlier = slot[None, :] < slot[:, None]
    repeat = jnp.any((lists[:, :, None] == lists[:, None, :]) & earlier[None], axis=2)
    keep = (slot[None, :] < counts[:, None]) & ~repeat
    place = jnp.sum(jnp.where(earlier[None], keep[:, None, :].astype(jnp.int32), 0), axis=2)
    chosen = keep[:, :, None] & (place[:, :, None] == slot[None, None, :])
    packed = jnp.sum(jnp.where(chosen, lists[:, :, None], 0), axis=1)
    lives = jnp.sum(keep.astype(jnp.int32), axis=1)
    block = jnp.arange(rows, dtype=jnp.int32)
    ahead = (lives[None, :] > lives[:, None]) | (
        (lives[None, :] == lives[:, None]) & (block[None, :] < block[:, None])
    )
    rank = jnp.sum(ahead.astype(jnp.int32), axis=1)
    order = jnp.sum(jnp.where(rank[:, None] == block[None, :], block[:, None], 0), axis=0)
    return packed, lives, order


def on_device(queries, keys_in, values, d_out, pair_blocks, pair_count):
    group = ("inner", "head")
    peers = lax.axis_size("inner") * lax.axis_size("head")
    outer = lax.axis_size("outer")
    tokens_dev, features = queries.shape
    tokens = tokens_dev * peers
    halo = REACH * (tokens // PERSONS_GROUP)
    blocks, halo_blocks = tokens // BLOCK, halo // BLOCK

    def exchange(parts):
        return lax.all_to_all(parts, group, split_axis=0, concat_axis=0, tiled=True)

    me = lax.axis_index(group)
    my_slab = me.astype(jnp.int32).reshape(1)
    half = peers // 2

    def send(slab, k):
        return lax.ppermute(slab, group, [(i, i ^ k) for i in range(peers)])

    def scatter(slabs):
        moved = {k: send(slabs[k], k) for k in SENDS}
        return [slabs[0]] + [moved[k] for k in range(1, peers)]

    def beside(slabs, lower, upper):
        pairs = [
            (o * peers + i, (o + (lower if i < half else upper)) * peers + i)
            for o in range(outer)
            for i in range(peers)
            if 0 <= o + (lower if i < half else upper) < outer
        ]
        return lax.ppermute(slabs, ("outer",) + group, pairs)

    up = [(i, i + 1) for i in range(outer - 1)]
    down = [(i + 1, i) for i in range(outer - 1)]
    own = scatter(join_columns(my_slab, keys_in, values, peers))
    qd = scatter(join_columns(my_slab, queries, d_out, peers))
    near = beside(jnp.stack(own[:half]), -1, 1)
    across = beside(jnp.stack(own[half:]), 1, -1)
    first = lax.axis_index("outer") * blocks
    lists, counts, order = compact_lists(
        pair_blocks, pair_count, first, blocks, first - halo_blocks, blocks + 2 * halo_blocks
    )
    qd, own = ([slabs[k] for k in (0,) + SENDS] for slabs in (qd, own))
    dq, grad_left, grad_own, grad_right = attend(
        my_slab, lists, counts, order, qd, own, near, across
    )
    from_above = lax.ppermute(grad_left, "outer", down)
    from_below = lax.ppermute(grad_right, "outer", up)
    dq_back = exchange(dq)
    arrived = jnp.concatenate([from_below, from_above], axis=0)
    total = (grad_own.astype(jnp.float32) + arrived.astype(jnp.float32)).astype(jnp.bfloat16)
    grads = exchange(total.reshape(peers, tokens_dev, 2 * LANES))

    def columns(parts):
        return parts.transpose(1, 0, 2).reshape(tokens_dev, features)

    return columns(dq_back), columns(grads[:, :, :LANES]), columns(grads[:, :, LANES:])


def solution(mesh):
    ctx, head = mesh.devices.shape
    grouped = Mesh(
        mesh.devices.reshape(ctx // PERSONS_GROUP, PERSONS_GROUP, head), ("outer", "inner", "head")
    )
    rows = P(("outer", "inner", "head"), None)
    return jax.shard_map(
        on_device,
        mesh=grouped,
        in_specs=(rows, rows, rows, rows, P(), P()),
        out_specs=(rows, rows, rows),
        check_vma=False,
    )
```

```python
import jax
import jax.numpy as jnp
from jax import lax
from jax.experimental import pallas as pl
from jax.experimental.pallas import tpu as pltpu
from jax.sharding import Mesh
from jax.sharding import PartitionSpec as P

HEAD_DIM = 64
BLOCK = 64
REACH = 2
PERSONS_GROUP = 4
CHUNK = 4
STEP = 4
SENDS = (2, 5, 4, 1, 7, 6, 3)
VMEM_BYTES = 63 * 1024 * 1024
LANES = 2 * HEAD_DIM
masked_value = -1e30


def dot_f32(lhs, rhs, lhs_dim, rhs_dim):
    return lax.dot_general(
        lhs, rhs, (((lhs_dim,), (rhs_dim,)), ((), ())), preferred_element_type=jnp.float32
    )


def mixed_rows(rows, mixer):
    return jnp.concatenate([rows] * 4, axis=0) * mixer[...]


def masked_softmax(both, live, slots, sure):
    biases = [jnp.where(slot < live, 0.0, masked_value) for slot in range(sure, slots)]
    scores = jnp.concatenate(
        [both[: sure * BLOCK, :LANES]]
        + [
            both[(sure + i) * BLOCK : (sure + i + 1) * BLOCK, :LANES] + bias
            for i, bias in enumerate(biases)
        ],
        axis=0,
    )
    d_probs = both[:, LANES:]
    top = jnp.max(scores, axis=0, keepdims=True)
    weights = jnp.exp(scores - top)
    inverse = 1.0 / jnp.sum(weights, axis=0, keepdims=True)
    delta = jnp.sum(weights * d_probs, axis=0, keepdims=True) * inverse
    probs = weights * inverse
    d_scores = probs * (d_probs - delta)
    return d_scores.astype(jnp.bfloat16), probs.astype(jnp.bfloat16)


def attend_step(slots, blocks, lives, lists_ref, qd, kv, acc, mixer, dq):
    rows = [pl.ds(pl.multiple_of(block * BLOCK, BLOCK), BLOCK) for block in blocks]
    places = [
        [
            pl.ds(pl.multiple_of(lists_ref[block, slot] * BLOCK, BLOCK), BLOCK)
            for slot in range(slots)
        ]
        for block in blocks
    ]
    weights = [mixed_rows(qd[row, :], mixer) for row in rows]
    windows = [jnp.concatenate([kv[place, :] for place in spot], axis=0) for spot in places]
    both = [dot_f32(window, weight, 1, 1) for window, weight in zip(windows, weights)]
    sures = [slots - CHUNK + 1] + [1] * (len(blocks) - 1)
    graded = [masked_softmax(b, live, slots, sure) for b, live, sure in zip(both, lives, sures)]
    grads = [
        dot_f32(jnp.concatenate([d_scores, probs], axis=1), weight, 1, 0)
        for (d_scores, probs), weight in zip(graded, weights)
    ]
    turned = [
        dot_f32(d_scores, window[:, :LANES], 0, 0)
        for (d_scores, _), window in zip(graded, windows)
    ]
    lane = lax.broadcasted_iota(jnp.int32, (BLOCK, LANES), 1)
    for row, both_heads in zip(rows, turned):
        picked = jnp.where(lane < HEAD_DIM, both_heads[:BLOCK], both_heads[BLOCK:])
        dq[row, :] = (picked * HEAD_DIM**-0.5).astype(jnp.bfloat16)
    for spot, grad in zip(places, grads):
        for slot, place in enumerate(spot):
            acc[place, :] += grad[slot * BLOCK : (slot + 1) * BLOCK]


def attend_kernel(
    me_ref, lists_ref, counts_ref, order_ref, *refs
):
    peers = len(refs) // 2 - 7
    qd_refs, own_refs = refs[:peers], refs[peers : 2 * peers]
    near_ref, across_ref, dq_ref, grad_left, grad_own, grad_right = refs[2 * peers : 2 * peers + 6]
    qd, kv, acc, mixer, dq, in_sems, sems, dq_sems = refs[2 * peers + 6 :]
    pairs = lists_ref.shape[1]
    halo, own = grad_left.shape[0], grad_own.shape[0]
    spots = [pl.ds(0, halo), pl.ds(halo, own), pl.ds(halo + own, halo)]
    me = me_ref[0]
    piece = own_refs[0].shape[0]
    edge = halo // piece
    lower = me < edge

    def rows_at(base, slab):
        return pl.ds(pl.multiple_of(base + slab * piece, piece), piece)

    copies = []
    for place, k in enumerate((0,) + SENDS):
        spot = rows_at(0, me ^ k)
        copies.append(pltpu.make_async_copy(qd_refs[place], qd.at[spot, :], in_sems.at[0, k]))
        spot = rows_at(halo, me ^ k)
        copies.append(pltpu.make_async_copy(own_refs[place], kv.at[spot, :], in_sems.at[1, k]))
    for k in range(edge):
        spot = rows_at(jnp.where(lower, halo + own, 0), (me ^ k) % edge)
        copies.append(pltpu.make_async_copy(near_ref.at[k], kv.at[spot, :], in_sems.at[2, k]))
        spot = rows_at(jnp.where(lower, 0, halo + own), (me ^ k) % edge)
        copies.append(
            pltpu.make_async_copy(across_ref.at[k], kv.at[spot, :], in_sems.at[2, edge + k])
        )
    for copy in copies:
        copy.start()
    acc[...] = jnp.zeros_like(acc)
    group_row = lax.broadcasted_iota(jnp.int32, mixer.shape, 0) // HEAD_DIM
    group_lane = lax.broadcasted_iota(jnp.int32, mixer.shape, 1) // HEAD_DIM
    scale = jnp.where(group_row < 2, HEAD_DIM**-0.5, 1.0)
    mixer[...] = jnp.where(group_row == group_lane, scale, 0.0).astype(jnp.bfloat16)
    for copy in copies:
        copy.wait()

    def one_step(step, carry):
        blocks = [order_ref[STEP * step + i] for i in range(STEP)]
        lives = [counts_ref[block] for block in blocks]
        for chunks in range(1, pairs // CHUNK + 1):

            @pl.when((lives[0] + CHUNK - 1) // CHUNK == chunks)
            def _():
                attend_step(chunks * CHUNK, blocks, lives, lists_ref, qd, kv, acc, mixer, dq)

        return carry

    lax.fori_loop(0, counts_ref.shape[0] // STEP, one_step, 0)
    rows = dq_ref.shape[1]
    backs = [
        pltpu.make_async_copy(dq.at[pl.ds(i * rows, rows), :], dq_ref.at[i], dq_sems.at[i])
        for i in range(peers)
    ]
    for back in backs:
        back.start()
    for i, (spot, ref) in enumerate(zip(spots, (grad_left, grad_own, grad_right))):
        kv[spot, :] = acc[spot, :].astype(jnp.bfloat16)
        back = pltpu.make_async_copy(kv.at[spot, :], ref, sems.at[i])
        back.start()
        backs.append(back)
    for back in backs:
        back.wait()


def attend(me, lists, counts, order, qd, own, near, across):
    peers, piece = len(own), own[0].shape[0]
    rows, halo = peers * piece, near.shape[0] * piece
    window = rows + 2 * halo
    scalars = pl.BlockSpec(memory_space=pltpu.SMEM)
    far = pl.BlockSpec(memory_space=pl.ANY)

    def shaped(shape):
        return jax.ShapeDtypeStruct(shape, jnp.bfloat16)

    return pl.pallas_call(
        attend_kernel,
        out_shape=(
            shaped((peers, rows // peers, LANES)),
            shaped((halo, 2 * LANES)),
            shaped((rows, 2 * LANES)),
            shaped((halo, 2 * LANES)),
        ),
        in_specs=[scalars] * 4 + [far] * (2 * peers + 2),
        out_specs=(far, far, far, far),
        scratch_shapes=[
            pltpu.VMEM((rows, 2 * LANES), jnp.bfloat16),
            pltpu.VMEM((window, 2 * LANES), jnp.bfloat16),
            pltpu.VMEM((window, 2 * LANES), jnp.float32),
            pltpu.VMEM((2 * LANES, 2 * LANES), jnp.bfloat16),
            pltpu.VMEM((rows, LANES), jnp.bfloat16),
            pltpu.SemaphoreType.DMA((3, peers)),
            pltpu.SemaphoreType.DMA((3,)),
            pltpu.SemaphoreType.DMA((peers,)),
        ],
        compiler_params=pltpu.CompilerParams(vmem_limit_bytes=VMEM_BYTES),
        cost_estimate=pl.CostEstimate(
            flops=4_000_000_000, bytes_accessed=6_000_000, transcendentals=2_000_000
        ),
        name="attend",
    )(me, lists, counts, order, *qd, *own, near, across)


def pack_kernel(me_ref, first_ref, second_ref, *refs):
    joined_refs, (packed, in_sems, out_sems) = refs[:-3], refs[-3:]
    peers, _, width = packed.shape
    width = width // 2
    me = me_ref[0]
    arriving = [
        [
            pltpu.make_async_copy(
                ref.at[:, pl.ds(pl.multiple_of((me ^ slab) * width, width), width)],
                packed.at[slab, :, pl.ds(half * width, width)],
                in_sems.at[slab, half],
            )
            for half, ref in enumerate((first_ref, second_ref))
        ]
        for slab in range(peers)
    ]
    leaving = [
        pltpu.make_async_copy(packed.at[slab], joined_refs[slab], out_sems.at[slab])
        for slab in range(peers)
    ]
    for halves in arriving:
        for copy in halves:
            copy.start()
    for halves, out in zip(arriving, leaving):
        for copy in halves:
            copy.wait()
        out.start()
    for out in leaving:
        out.wait()


def join_columns(me, first, second, peers):
    rows, features = first.shape
    shape = (peers, rows, 2 * features // peers)
    anywhere = pl.BlockSpec(memory_space=pl.ANY)
    slab = jax.ShapeDtypeStruct(shape[1:], first.dtype)
    return pl.pallas_call(
        pack_kernel,
        out_shape=[slab] * peers,
        in_specs=[pl.BlockSpec(memory_space=pltpu.SMEM), anywhere, anywhere],
        out_specs=[anywhere] * peers,
        scratch_shapes=[
            pltpu.VMEM(shape, first.dtype),
            pltpu.SemaphoreType.DMA((peers, 2)),
            pltpu.SemaphoreType.DMA((peers,)),
        ],
        cost_estimate=pl.CostEstimate(flops=0, bytes_accessed=2_000_000, transcendentals=0),
        name="pack",
    )(me, first, second)


def compact_lists(pair_blocks, pair_count, first, rows, lowest, window_blocks):
    lists = lax.dynamic_slice_in_dim(pair_blocks, first, rows, 0) - lowest
    lists = jnp.clip(lists, 0, window_blocks - 1)
    counts = lax.dynamic_slice_in_dim(pair_count, first, rows, 0)
    slot = jnp.arange(lists.shape[1], dtype=jnp.int32)
    earlier = slot[None, :] < slot[:, None]
    repeat = jnp.any((lists[:, :, None] == lists[:, None, :]) & earlier[None], axis=2)
    keep = (slot[None, :] < counts[:, None]) & ~repeat
    place = jnp.sum(jnp.where(earlier[None], keep[:, None, :].astype(jnp.int32), 0), axis=2)
    chosen = keep[:, :, None] & (place[:, :, None] == slot[None, None, :])
    packed = jnp.sum(jnp.where(chosen, lists[:, :, None], 0), axis=1)
    lives = jnp.sum(keep.astype(jnp.int32), axis=1)
    block = jnp.arange(rows, dtype=jnp.int32)
    ahead = (lives[None, :] > lives[:, None]) | (
        (lives[None, :] == lives[:, None]) & (block[None, :] < block[:, None])
    )
    rank = jnp.sum(ahead.astype(jnp.int32), axis=1)
    order = jnp.sum(jnp.where(rank[:, None] == block[None, :], block[:, None], 0), axis=0)
    return packed, lives, order


def on_device(queries, keys_in, values, d_out, pair_blocks, pair_count):
    group = ("inner", "head")
    peers = lax.axis_size("inner") * lax.axis_size("head")
    outer = lax.axis_size("outer")
    tokens_dev, features = queries.shape
    tokens = tokens_dev * peers
    halo = REACH * (tokens // PERSONS_GROUP)
    blocks, halo_blocks = tokens // BLOCK, halo // BLOCK

    def exchange(parts):
        return lax.all_to_all(parts, group, split_axis=0, concat_axis=0, tiled=True)

    me = lax.axis_index(group)
    my_slab = me.astype(jnp.int32).reshape(1)
    half = peers // 2

    def send(slab, k):
        return lax.ppermute(slab, group, [(i, i ^ k) for i in range(peers)])

    def scatter(slabs):
        moved = {k: send(slabs[k], k) for k in SENDS}
        return [slabs[0]] + [moved[k] for k in range(1, peers)]

    def beside(slabs, lower, upper):
        pairs = [
            (o * peers + i, (o + (lower if i < half else upper)) * peers + i)
            for o in range(outer)
            for i in range(peers)
            if 0 <= o + (lower if i < half else upper) < outer
        ]
        return lax.ppermute(slabs, ("outer",) + group, pairs)

    up = [(i, i + 1) for i in range(outer - 1)]
    down = [(i + 1, i) for i in range(outer - 1)]
    own = scatter(join_columns(my_slab, keys_in, values, peers))
    qd = scatter(join_columns(my_slab, queries, d_out, peers))
    near = beside(jnp.stack(own[:half]), -1, 1)
    across = beside(jnp.stack(own[half:]), 1, -1)
    first = lax.axis_index("outer") * blocks
    lists, counts, order = compact_lists(
        pair_blocks, pair_count, first, blocks, first - halo_blocks, blocks + 2 * halo_blocks
    )
    qd, own = ([slabs[k] for k in (0,) + SENDS] for slabs in (qd, own))
    dq, grad_left, grad_own, grad_right = attend(
        my_slab, lists, counts, order, qd, own, near, across
    )
    from_above = lax.ppermute(grad_left, "outer", down)
    from_below = lax.ppermute(grad_right, "outer", up)
    dq_back = exchange(dq)
    arrived = jnp.concatenate([from_below, from_above], axis=0)
    total = (grad_own.astype(jnp.float32) + arrived.astype(jnp.float32)).astype(jnp.bfloat16)
    grads = exchange(total.reshape(peers, tokens_dev, 2 * LANES))

    def columns(parts):
        return parts.transpose(1, 0, 2).reshape(tokens_dev, features)

    return columns(dq_back), columns(grads[:, :, :LANES]), columns(grads[:, :, LANES:])


def solution(mesh):
    ctx, head = mesh.devices.shape
    grouped = Mesh(
        mesh.devices.reshape(ctx // PERSONS_GROUP, PERSONS_GROUP, head), ("outer", "inner", "head")
    )
    rows = P(("outer", "inner", "head"), None)
    return jax.shard_map(
        on_device,
        mesh=grouped,
        in_specs=(rows, rows, rows, rows, P(), P()),
        out_specs=(rows, rows, rows),
        check_vma=False,
    )
```

```python
import jax
import jax.numpy as jnp
from jax import lax
from jax.experimental import pallas as pl
from jax.experimental.pallas import tpu as pltpu
from jax.sharding import Mesh
from jax.sharding import PartitionSpec as P

HEAD_DIM = 64
BLOCK = 64
REACH = 2
PERSONS_GROUP = 4
CHUNK = 4
STEP = 4
SENDS = (4, 1, 5, 7, 3, 6, 2)
VMEM_BYTES = 63 * 1024 * 1024
LANES = 2 * HEAD_DIM
masked_value = -1e30


def dot_f32(lhs, rhs, lhs_dim, rhs_dim):
    return lax.dot_general(
        lhs, rhs, (((lhs_dim,), (rhs_dim,)), ((), ())), preferred_element_type=jnp.float32
    )


def mixed_rows(rows, mixer):
    return jnp.concatenate([rows] * 4, axis=0) * mixer[...]


def masked_softmax(both, live, slots, sure):
    biases = [jnp.where(slot < live, 0.0, masked_value) for slot in range(sure, slots)]
    scores = jnp.concatenate(
        [both[: sure * BLOCK, :LANES]]
        + [
            both[(sure + i) * BLOCK : (sure + i + 1) * BLOCK, :LANES] + bias
            for i, bias in enumerate(biases)
        ],
        axis=0,
    )
    d_probs = both[:, LANES:]
    top = jnp.max(scores, axis=0, keepdims=True)
    weights = jnp.exp(scores - top)
    inverse = 1.0 / jnp.sum(weights, axis=0, keepdims=True)
    delta = jnp.sum(weights * d_probs, axis=0, keepdims=True) * inverse
    probs = weights * inverse
    d_scores = probs * (d_probs - delta)
    return d_scores.astype(jnp.bfloat16), probs.astype(jnp.bfloat16)


def attend_step(slots, blocks, lives, lists_ref, qd, kv, acc, mixer, dq):
    rows = [pl.ds(pl.multiple_of(block * BLOCK, BLOCK), BLOCK) for block in blocks]
    places = [
        [
            pl.ds(pl.multiple_of(lists_ref[block, slot] * BLOCK, BLOCK), BLOCK)
            for slot in range(slots)
        ]
        for block in blocks
    ]
    weights = [mixed_rows(qd[row, :], mixer) for row in rows]
    windows = [jnp.concatenate([kv[place, :] for place in spot], axis=0) for spot in places]
    both = [dot_f32(window, weight, 1, 1) for window, weight in zip(windows, weights)]
    sures = [slots - CHUNK + 1] + [1] * (len(blocks) - 1)
    graded = [masked_softmax(b, live, slots, sure) for b, live, sure in zip(both, lives, sures)]
    grads = [
        dot_f32(jnp.concatenate([d_scores, probs], axis=1), weight, 1, 0)
        for (d_scores, probs), weight in zip(graded, weights)
    ]
    turned = [
        dot_f32(d_scores, window[:, :LANES], 0, 0)
        for (d_scores, _), window in zip(graded, windows)
    ]
    lane = lax.broadcasted_iota(jnp.int32, (BLOCK, LANES), 1)
    for row, both_heads in zip(rows, turned):
        picked = jnp.where(lane < HEAD_DIM, both_heads[:BLOCK], both_heads[BLOCK:])
        dq[row, :] = (picked * HEAD_DIM**-0.5).astype(jnp.bfloat16)
    for spot, grad in zip(places, grads):
        for slot, place in enumerate(spot):
            acc[place, :] += grad[slot * BLOCK : (slot + 1) * BLOCK]


def attend_kernel(
    me_ref, lists_ref, counts_ref, order_ref, *refs
):
    peers = len(refs) // 2 - 7
    qd_refs, own_refs = refs[:peers], refs[peers : 2 * peers]
    near_ref, across_ref, dq_ref, grad_left, grad_own, grad_right = refs[2 * peers : 2 * peers + 6]
    qd, kv, acc, mixer, dq, in_sems, sems, dq_sems = refs[2 * peers + 6 :]
    pairs = lists_ref.shape[1]
    halo, own = grad_left.shape[0], grad_own.shape[0]
    spots = [pl.ds(0, halo), pl.ds(halo, own), pl.ds(halo + own, halo)]
    me = me_ref[0]
    piece = own_refs[0].shape[0]
    edge = halo // piece
    lower = me < edge

    def rows_at(base, slab):
        return pl.ds(pl.multiple_of(base + slab * piece, piece), piece)

    copies = []
    for place, k in enumerate((0,) + SENDS):
        spot = rows_at(0, me ^ k)
        copies.append(pltpu.make_async_copy(qd_refs[place], qd.at[spot, :], in_sems.at[0, k]))
        spot = rows_at(halo, me ^ k)
        copies.append(pltpu.make_async_copy(own_refs[place], kv.at[spot, :], in_sems.at[1, k]))
    for k in range(edge):
        spot = rows_at(jnp.where(lower, halo + own, 0), (me ^ k) % edge)
        copies.append(pltpu.make_async_copy(near_ref.at[k], kv.at[spot, :], in_sems.at[2, k]))
        spot = rows_at(jnp.where(lower, 0, halo + own), (me ^ k) % edge)
        copies.append(
            pltpu.make_async_copy(across_ref.at[k], kv.at[spot, :], in_sems.at[2, edge + k])
        )
    for copy in copies:
        copy.start()
    acc[...] = jnp.zeros_like(acc)
    group_row = lax.broadcasted_iota(jnp.int32, mixer.shape, 0) // HEAD_DIM
    group_lane = lax.broadcasted_iota(jnp.int32, mixer.shape, 1) // HEAD_DIM
    scale = jnp.where(group_row < 2, HEAD_DIM**-0.5, 1.0)
    mixer[...] = jnp.where(group_row == group_lane, scale, 0.0).astype(jnp.bfloat16)
    for copy in copies:
        copy.wait()

    def one_step(step, carry):
        blocks = [order_ref[STEP * step + i] for i in range(STEP)]
        lives = [counts_ref[block] for block in blocks]
        for chunks in range(1, pairs // CHUNK + 1):

            @pl.when((lives[0] + CHUNK - 1) // CHUNK == chunks)
            def _():
                attend_step(chunks * CHUNK, blocks, lives, lists_ref, qd, kv, acc, mixer, dq)

        return carry

    lax.fori_loop(0, counts_ref.shape[0] // STEP, one_step, 0)
    rows = dq_ref.shape[1]
    backs = [
        pltpu.make_async_copy(dq.at[pl.ds(i * rows, rows), :], dq_ref.at[i], dq_sems.at[i])
        for i in range(peers)
    ]
    for back in backs:
        back.start()
    for i, (spot, ref) in enumerate(zip(spots, (grad_left, grad_own, grad_right))):
        kv[spot, :] = acc[spot, :].astype(jnp.bfloat16)
        back = pltpu.make_async_copy(kv.at[spot, :], ref, sems.at[i])
        back.start()
        backs.append(back)
    for back in backs:
        back.wait()


def attend(me, lists, counts, order, qd, own, near, across):
    peers, piece = len(own), own[0].shape[0]
    rows, halo = peers * piece, near.shape[0] * piece
    window = rows + 2 * halo
    scalars = pl.BlockSpec(memory_space=pltpu.SMEM)
    far = pl.BlockSpec(memory_space=pl.ANY)

    def shaped(shape):
        return jax.ShapeDtypeStruct(shape, jnp.bfloat16)

    return pl.pallas_call(
        attend_kernel,
        out_shape=(
            shaped((peers, rows // peers, LANES)),
            shaped((halo, 2 * LANES)),
            shaped((rows, 2 * LANES)),
            shaped((halo, 2 * LANES)),
        ),
        in_specs=[scalars] * 4 + [far] * (2 * peers + 2),
        out_specs=(far, far, far, far),
        scratch_shapes=[
            pltpu.VMEM((rows, 2 * LANES), jnp.bfloat16),
            pltpu.VMEM((window, 2 * LANES), jnp.bfloat16),
            pltpu.VMEM((window, 2 * LANES), jnp.float32),
            pltpu.VMEM((2 * LANES, 2 * LANES), jnp.bfloat16),
            pltpu.VMEM((rows, LANES), jnp.bfloat16),
            pltpu.SemaphoreType.DMA((3, peers)),
            pltpu.SemaphoreType.DMA((3,)),
            pltpu.SemaphoreType.DMA((peers,)),
        ],
        compiler_params=pltpu.CompilerParams(vmem_limit_bytes=VMEM_BYTES),
        cost_estimate=pl.CostEstimate(
            flops=4_000_000_000, bytes_accessed=6_000_000, transcendentals=2_000_000
        ),
        name="attend",
    )(me, lists, counts, order, *qd, *own, near, across)


def pack_kernel(me_ref, first_ref, second_ref, *refs):
    joined_refs, (packed, in_sems, out_sems) = refs[:-3], refs[-3:]
    peers, _, width = packed.shape
    width = width // 2
    me = me_ref[0]
    arriving = [
        [
            pltpu.make_async_copy(
                ref.at[:, pl.ds(pl.multiple_of((me ^ slab) * width, width), width)],
                packed.at[slab, :, pl.ds(half * width, width)],
                in_sems.at[slab, half],
            )
            for half, ref in enumerate((first_ref, second_ref))
        ]
        for slab in range(peers)
    ]
    leaving = [
        pltpu.make_async_copy(packed.at[slab], joined_refs[slab], out_sems.at[slab])
        for slab in range(peers)
    ]
    for halves in arriving:
        for copy in halves:
            copy.start()
    for halves, out in zip(arriving, leaving):
        for copy in halves:
            copy.wait()
        out.start()
    for out in leaving:
        out.wait()


def join_columns(me, first, second, peers):
    rows, features = first.shape
    shape = (peers, rows, 2 * features // peers)
    anywhere = pl.BlockSpec(memory_space=pl.ANY)
    slab = jax.ShapeDtypeStruct(shape[1:], first.dtype)
    return pl.pallas_call(
        pack_kernel,
        out_shape=[slab] * peers,
        in_specs=[pl.BlockSpec(memory_space=pltpu.SMEM), anywhere, anywhere],
        out_specs=[anywhere] * peers,
        scratch_shapes=[
            pltpu.VMEM(shape, first.dtype),
            pltpu.SemaphoreType.DMA((peers, 2)),
            pltpu.SemaphoreType.DMA((peers,)),
        ],
        cost_estimate=pl.CostEstimate(flops=0, bytes_accessed=2_000_000, transcendentals=0),
        name="pack",
    )(me, first, second)


def compact_lists(pair_blocks, pair_count, first, rows, lowest, window_blocks):
    lists = lax.dynamic_slice_in_dim(pair_blocks, first, rows, 0) - lowest
    lists = jnp.clip(lists, 0, window_blocks - 1)
    counts = lax.dynamic_slice_in_dim(pair_count, first, rows, 0)
    slot = jnp.arange(lists.shape[1], dtype=jnp.int32)
    earlier = slot[None, :] < slot[:, None]
    repeat = jnp.any((lists[:, :, None] == lists[:, None, :]) & earlier[None], axis=2)
    keep = (slot[None, :] < counts[:, None]) & ~repeat
    place = jnp.sum(jnp.where(earlier[None], keep[:, None, :].astype(jnp.int32), 0), axis=2)
    chosen = keep[:, :, None] & (place[:, :, None] == slot[None, None, :])
    packed = jnp.sum(jnp.where(chosen, lists[:, :, None], 0), axis=1)
    lives = jnp.sum(keep.astype(jnp.int32), axis=1)
    block = jnp.arange(rows, dtype=jnp.int32)
    ahead = (lives[None, :] > lives[:, None]) | (
        (lives[None, :] == lives[:, None]) & (block[None, :] < block[:, None])
    )
    rank = jnp.sum(ahead.astype(jnp.int32), axis=1)
    order = jnp.sum(jnp.where(rank[:, None] == block[None, :], block[:, None], 0), axis=0)
    return packed, lives, order


def on_device(queries, keys_in, values, d_out, pair_blocks, pair_count):
    group = ("inner", "head")
    peers = lax.axis_size("inner") * lax.axis_size("head")
    outer = lax.axis_size("outer")
    tokens_dev, features = queries.shape
    tokens = tokens_dev * peers
    halo = REACH * (tokens // PERSONS_GROUP)
    blocks, halo_blocks = tokens // BLOCK, halo // BLOCK

    def exchange(parts):
        return lax.all_to_all(parts, group, split_axis=0, concat_axis=0, tiled=True)

    me = lax.axis_index(group)
    my_slab = me.astype(jnp.int32).reshape(1)
    half = peers // 2

    def send(slab, k):
        return lax.ppermute(slab, group, [(i, i ^ k) for i in range(peers)])

    def scatter(slabs):
        moved = {k: send(slabs[k], k) for k in SENDS}
        return [slabs[0]] + [moved[k] for k in range(1, peers)]

    def beside(slabs, lower, upper):
        pairs = [
            (o * peers + i, (o + (lower if i < half else upper)) * peers + i)
            for o in range(outer)
            for i in range(peers)
            if 0 <= o + (lower if i < half else upper) < outer
        ]
        return lax.ppermute(slabs, ("outer",) + group, pairs)

    up = [(i, i + 1) for i in range(outer - 1)]
    down = [(i + 1, i) for i in range(outer - 1)]
    own = scatter(join_columns(my_slab, keys_in, values, peers))
    qd = scatter(join_columns(my_slab, queries, d_out, peers))
    near = beside(jnp.stack(own[:half]), -1, 1)
    across = beside(jnp.stack(own[half:]), 1, -1)
    first = lax.axis_index("outer") * blocks
    lists, counts, order = compact_lists(
        pair_blocks, pair_count, first, blocks, first - halo_blocks, blocks + 2 * halo_blocks
    )
    qd, own = ([slabs[k] for k in (0,) + SENDS] for slabs in (qd, own))
    dq, grad_left, grad_own, grad_right = attend(
        my_slab, lists, counts, order, qd, own, near, across
    )
    from_above = lax.ppermute(grad_left, "outer", down)
    from_below = lax.ppermute(grad_right, "outer", up)
    dq_back = exchange(dq)
    arrived = jnp.concatenate([from_below, from_above], axis=0)
    total = (grad_own.astype(jnp.float32) + arrived.astype(jnp.float32)).astype(jnp.bfloat16)
    grads = exchange(total.reshape(peers, tokens_dev, 2 * LANES))

    def columns(parts):
        return parts.transpose(1, 0, 2).reshape(tokens_dev, features)

    return columns(dq_back), columns(grads[:, :, :LANES]), columns(grads[:, :, LANES:])


def solution(mesh):
    ctx, head = mesh.devices.shape
    grouped = Mesh(
        mesh.devices.reshape(ctx // PERSONS_GROUP, PERSONS_GROUP, head), ("outer", "inner", "head")
    )
    rows = P(("outer", "inner", "head"), None)
    return jax.shard_map(
        on_device,
        mesh=grouped,
        in_specs=(rows, rows, rows, rows, P(), P()),
        out_specs=(rows, rows, rows),
        check_vma=False,
    )
```

```python
import jax
import jax.numpy as jnp
from jax import lax
from jax.experimental import pallas as pl
from jax.experimental.pallas import tpu as pltpu
from jax.sharding import Mesh
from jax.sharding import PartitionSpec as P

HEAD_DIM = 64
BLOCK = 64
REACH = 2
PERSONS_GROUP = 4
CHUNK = 4
STEP = 4
SENDS = (4, 1, 5, 7, 3, 6, 2)
VMEM_BYTES = 63 * 1024 * 1024
LANES = 2 * HEAD_DIM
masked_value = -1e30


def dot_f32(lhs, rhs, lhs_dim, rhs_dim):
    return lax.dot_general(
        lhs, rhs, (((lhs_dim,), (rhs_dim,)), ((), ())), preferred_element_type=jnp.float32
    )


def mixed_rows(rows, mixer):
    return jnp.concatenate([rows] * 4, axis=0) * mixer[...]


def masked_softmax(both, live, slots, sure):
    biases = [jnp.where(slot < live, 0.0, masked_value) for slot in range(sure, slots)]
    scores = jnp.concatenate(
        [both[: sure * BLOCK, :LANES]]
        + [
            both[(sure + i) * BLOCK : (sure + i + 1) * BLOCK, :LANES] + bias
            for i, bias in enumerate(biases)
        ],
        axis=0,
    )
    d_probs = both[:, LANES:]
    top = jnp.max(scores, axis=0, keepdims=True)
    weights = jnp.exp(scores - top)
    inverse = 1.0 / jnp.sum(weights, axis=0, keepdims=True)
    delta = jnp.sum(weights * d_probs, axis=0, keepdims=True) * inverse
    probs = weights * inverse
    d_scores = probs * (d_probs - delta)
    return d_scores.astype(jnp.bfloat16), probs.astype(jnp.bfloat16)


def attend_step(slots, blocks, lives, lists_ref, qd, kv, acc, mixer, dq):
    rows = [pl.ds(pl.multiple_of(block * BLOCK, BLOCK), BLOCK) for block in blocks]
    places = [
        [
            pl.ds(pl.multiple_of(lists_ref[block, slot] * BLOCK, BLOCK), BLOCK)
            for slot in range(slots)
        ]
        for block in blocks
    ]
    weights = [mixed_rows(qd[row, :], mixer) for row in rows]
    windows = [jnp.concatenate([kv[place, :] for place in spot], axis=0) for spot in places]
    both = [dot_f32(window, weight, 1, 1) for window, weight in zip(windows, weights)]
    sures = [slots - CHUNK + 1] + [1] * (len(blocks) - 1)
    graded = [masked_softmax(b, live, slots, sure) for b, live, sure in zip(both, lives, sures)]
    grads = [
        dot_f32(jnp.concatenate([d_scores, probs], axis=1), weight, 1, 0)
        for (d_scores, probs), weight in zip(graded, weights)
    ]
    turned = [
        dot_f32(d_scores, window[:, :LANES], 0, 0)
        for (d_scores, _), window in zip(graded, windows)
    ]
    lane = lax.broadcasted_iota(jnp.int32, (BLOCK, LANES), 1)
    for row, both_heads in zip(rows, turned):
        picked = jnp.where(lane < HEAD_DIM, both_heads[:BLOCK], both_heads[BLOCK:])
        dq[row, :] = (picked * HEAD_DIM**-0.5).astype(jnp.bfloat16)
    for spot, grad in zip(places, grads):
        for slot, place in enumerate(spot):
            acc[place, :] += grad[slot * BLOCK : (slot + 1) * BLOCK]


def attend_kernel(
    me_ref, lists_ref, counts_ref, order_ref, *refs
):
    peers = len(refs) // 2 - 7
    qd_refs, own_refs = refs[:peers], refs[peers : 2 * peers]
    near_ref, across_ref, dq_ref, grad_left, grad_own, grad_right = refs[2 * peers : 2 * peers + 6]
    qd, kv, acc, mixer, dq, in_sems, sems, dq_sems = refs[2 * peers + 6 :]
    pairs = lists_ref.shape[1]
    halo, own = grad_left.shape[0], grad_own.shape[0]
    spots = [pl.ds(0, halo), pl.ds(halo, own), pl.ds(halo + own, halo)]
    me = me_ref[0]
    piece = own_refs[0].shape[0]
    edge = halo // piece
    lower = me < edge

    def rows_at(base, slab):
        return pl.ds(pl.multiple_of(base + slab * piece, piece), piece)

    copies = []
    for place, k in enumerate((0,) + SENDS):
        spot = rows_at(0, me ^ k)
        copies.append(pltpu.make_async_copy(qd_refs[place], qd.at[spot, :], in_sems.at[0, k]))
        spot = rows_at(halo, me ^ k)
        copies.append(pltpu.make_async_copy(own_refs[place], kv.at[spot, :], in_sems.at[1, k]))
    for k in range(edge):
        spot = rows_at(jnp.where(lower, halo + own, 0), (me ^ k) % edge)
        copies.append(pltpu.make_async_copy(near_ref.at[k], kv.at[spot, :], in_sems.at[2, k]))
        spot = rows_at(jnp.where(lower, 0, halo + own), (me ^ k) % edge)
        copies.append(
            pltpu.make_async_copy(across_ref.at[k], kv.at[spot, :], in_sems.at[2, edge + k])
        )
    for copy in copies:
        copy.start()
    acc[...] = jnp.zeros_like(acc)
    group_row = lax.broadcasted_iota(jnp.int32, mixer.shape, 0) // HEAD_DIM
    group_lane = lax.broadcasted_iota(jnp.int32, mixer.shape, 1) // HEAD_DIM
    scale = jnp.where(group_row < 2, HEAD_DIM**-0.5, 1.0)
    mixer[...] = jnp.where(group_row == group_lane, scale, 0.0).astype(jnp.bfloat16)
    for copy in copies:
        copy.wait()

    def one_step(step, carry):
        blocks = [order_ref[STEP * step + i] for i in range(STEP)]
        lives = [counts_ref[block] for block in blocks]
        for chunks in range(1, pairs // CHUNK + 1):

            @pl.when((lives[0] + CHUNK - 1) // CHUNK == chunks)
            def _():
                attend_step(chunks * CHUNK, blocks, lives, lists_ref, qd, kv, acc, mixer, dq)

        return carry

    lax.fori_loop(0, counts_ref.shape[0] // STEP, one_step, 0)
    rows = dq_ref.shape[1]
    backs = [
        pltpu.make_async_copy(dq.at[pl.ds(i * rows, rows), :], dq_ref.at[i], dq_sems.at[i])
        for i in range(peers)
    ]
    for back in backs:
        back.start()
    for i, (spot, ref) in enumerate(zip(spots, (grad_left, grad_own, grad_right))):
        kv[spot, :] = acc[spot, :].astype(jnp.bfloat16)
        back = pltpu.make_async_copy(kv.at[spot, :], ref, sems.at[i])
        back.start()
        backs.append(back)
    for back in backs:
        back.wait()


def attend(me, lists, counts, order, qd, own, near, across):
    peers, piece = len(own), own[0].shape[0]
    rows, halo = peers * piece, near.shape[0] * piece
    window = rows + 2 * halo
    scalars = pl.BlockSpec(memory_space=pltpu.SMEM)
    far = pl.BlockSpec(memory_space=pl.ANY)

    def shaped(shape):
        return jax.ShapeDtypeStruct(shape, jnp.bfloat16)

    return pl.pallas_call(
        attend_kernel,
        out_shape=(
            shaped((peers, rows // peers, LANES)),
            shaped((halo, 2 * LANES)),
            shaped((rows, 2 * LANES)),
            shaped((halo, 2 * LANES)),
        ),
        in_specs=[scalars] * 4 + [far] * (2 * peers + 2),
        out_specs=(far, far, far, far),
        scratch_shapes=[
            pltpu.VMEM((rows, 2 * LANES), jnp.bfloat16),
            pltpu.VMEM((window, 2 * LANES), jnp.bfloat16),
            pltpu.VMEM((window, 2 * LANES), jnp.float32),
            pltpu.VMEM((2 * LANES, 2 * LANES), jnp.bfloat16),
            pltpu.VMEM((rows, LANES), jnp.bfloat16),
            pltpu.SemaphoreType.DMA((3, peers)),
            pltpu.SemaphoreType.DMA((3,)),
            pltpu.SemaphoreType.DMA((peers,)),
        ],
        compiler_params=pltpu.CompilerParams(vmem_limit_bytes=VMEM_BYTES),
        cost_estimate=pl.CostEstimate(
            flops=4_000_000_000, bytes_accessed=6_000_000, transcendentals=2_000_000
        ),
        name="attend",
    )(me, lists, counts, order, *qd, *own, near, across)


def pack_kernel(me_ref, first_ref, second_ref, *refs):
    joined_refs, (packed, in_sems, out_sems) = refs[:-3], refs[-3:]
    peers, _, width = packed.shape
    width = width // 2
    me = me_ref[0]
    arriving = [
        [
            pltpu.make_async_copy(
                ref.at[:, pl.ds(pl.multiple_of((me ^ slab) * width, width), width)],
                packed.at[slab, :, pl.ds(half * width, width)],
                in_sems.at[slab, half],
            )
            for half, ref in enumerate((first_ref, second_ref))
        ]
        for slab in range(peers)
    ]
    leaving = [
        pltpu.make_async_copy(packed.at[slab], joined_refs[slab], out_sems.at[slab])
        for slab in range(peers)
    ]
    for halves in arriving:
        for copy in halves:
            copy.start()
    for halves, out in zip(arriving, leaving):
        for copy in halves:
            copy.wait()
        out.start()
    for out in leaving:
        out.wait()


def join_columns(me, first, second, peers):
    rows, features = first.shape
    shape = (peers, rows, 2 * features // peers)
    anywhere = pl.BlockSpec(memory_space=pl.ANY)
    slab = jax.ShapeDtypeStruct(shape[1:], first.dtype)
    return pl.pallas_call(
        pack_kernel,
        out_shape=[slab] * peers,
        in_specs=[pl.BlockSpec(memory_space=pltpu.SMEM), anywhere, anywhere],
        out_specs=[anywhere] * peers,
        scratch_shapes=[
            pltpu.VMEM(shape, first.dtype),
            pltpu.SemaphoreType.DMA((peers, 2)),
            pltpu.SemaphoreType.DMA((peers,)),
        ],
        cost_estimate=pl.CostEstimate(flops=0, bytes_accessed=2_000_000, transcendentals=0),
        name="pack",
    )(me, first, second)


def compact_lists(pair_blocks, pair_count, first, rows, lowest, window_blocks):
    lists = lax.dynamic_slice_in_dim(pair_blocks, first, rows, 0) - lowest
    lists = jnp.clip(lists, 0, window_blocks - 1)
    counts = lax.dynamic_slice_in_dim(pair_count, first, rows, 0)
    slot = jnp.arange(lists.shape[1], dtype=jnp.int32)
    earlier = slot[None, :] < slot[:, None]
    repeat = jnp.any((lists[:, :, None] == lists[:, None, :]) & earlier[None], axis=2)
    keep = (slot[None, :] < counts[:, None]) & ~repeat
    place = jnp.sum(jnp.where(earlier[None], keep[:, None, :].astype(jnp.int32), 0), axis=2)
    chosen = keep[:, :, None] & (place[:, :, None] == slot[None, None, :])
    packed = jnp.sum(jnp.where(chosen, lists[:, :, None], 0), axis=1)
    lives = jnp.sum(keep.astype(jnp.int32), axis=1)
    block = jnp.arange(rows, dtype=jnp.int32)
    ahead = (lives[None, :] > lives[:, None]) | (
        (lives[None, :] == lives[:, None]) & (block[None, :] < block[:, None])
    )
    rank = jnp.sum(ahead.astype(jnp.int32), axis=1)
    order = jnp.sum(jnp.where(rank[:, None] == block[None, :], block[:, None], 0), axis=0)
    return packed, lives, order


def on_device(queries, keys_in, values, d_out, pair_blocks, pair_count):
    group = ("inner", "head")
    peers = lax.axis_size("inner") * lax.axis_size("head")
    outer = lax.axis_size("outer")
    tokens_dev, features = queries.shape
    tokens = tokens_dev * peers
    halo = REACH * (tokens // PERSONS_GROUP)
    blocks, halo_blocks = tokens // BLOCK, halo // BLOCK

    def exchange(parts):
        return lax.all_to_all(parts, group, split_axis=0, concat_axis=0, tiled=True)

    me = lax.axis_index(group)
    my_slab = me.astype(jnp.int32).reshape(1)
    half = peers // 2

    def send(slab, k):
        return lax.ppermute(slab, group, [(i, i ^ k) for i in range(peers)])

    def scatter(slabs):
        moved = {k: send(slabs[k], k) for k in SENDS}
        return [slabs[0]] + [moved[k] for k in range(1, peers)]

    def beside(slabs, lower, upper):
        pairs = [
            (o * peers + i, (o + (lower if i < half else upper)) * peers + i)
            for o in range(outer)
            for i in range(peers)
            if 0 <= o + (lower if i < half else upper) < outer
        ]
        return lax.ppermute(slabs, ("outer",) + group, pairs)

    up = [(i, i + 1) for i in range(outer - 1)]
    down = [(i + 1, i) for i in range(outer - 1)]
    own = scatter(join_columns(my_slab, keys_in, values, peers))
    near, across = jnp.stack(own[:half]), jnp.stack(own[half:])
    qd = list(join_columns(my_slab, queries, d_out, peers))
    across, *held = lax.optimization_barrier([across] + [qd[k] for k in SENDS[1:]])
    for k, slab in zip(SENDS[1:], held):
        qd[k] = slab
    near, across = beside(near, -1, 1), beside(across, 1, -1)
    qd = scatter(qd)
    first = lax.axis_index("outer") * blocks
    lists, counts, order = compact_lists(
        pair_blocks, pair_count, first, blocks, first - halo_blocks, blocks + 2 * halo_blocks
    )
    qd, own = ([slabs[k] for k in (0,) + SENDS] for slabs in (qd, own))
    dq, grad_left, grad_own, grad_right = attend(
        my_slab, lists, counts, order, qd, own, near, across
    )
    from_above = lax.ppermute(grad_left, "outer", down)
    from_below = lax.ppermute(grad_right, "outer", up)
    dq_back = exchange(dq)
    arrived = jnp.concatenate([from_below, from_above], axis=0)
    total = (grad_own.astype(jnp.float32) + arrived.astype(jnp.float32)).astype(jnp.bfloat16)
    grads = exchange(total.reshape(peers, tokens_dev, 2 * LANES))

    def columns(parts):
        return parts.transpose(1, 0, 2).reshape(tokens_dev, features)

    return columns(dq_back), columns(grads[:, :, :LANES]), columns(grads[:, :, LANES:])


def solution(mesh):
    ctx, head = mesh.devices.shape
    grouped = Mesh(
        mesh.devices.reshape(ctx // PERSONS_GROUP, PERSONS_GROUP, head), ("outer", "inner", "head")
    )
    rows = P(("outer", "inner", "head"), None)
    return jax.shard_map(
        on_device,
        mesh=grouped,
        in_specs=(rows, rows, rows, rows, P(), P()),
        out_specs=(rows, rows, rows),
        check_vma=False,
    )
```
